32 devices in a mesh: grp: 2 (over y), tm: 8 (over z, x), inp: 2 (over core).
Axes of the slice: x: 2, y: 2, z: 4, core: 2. Of those that a mesh axis runs over, the one named last changes fastest.
Arguments:
- raw_samples: bfloat16 [4096, 16384], P(('grp', 'inp'), 'tm'), parts along dimension 0, may hold values from -24 to 24
- pfb_window: float32 [4, 2048], replicated, may hold values from -0.75 to 0.75
- tile_table: int32 [36, 2], P('inp'), may hold values from 0 to 7, as said below
Outputs:
- visibility: bfloat16 [128, 36, 2, 256, 256], P(('grp', 'tm'), 'inp'), parts along dimension 0
The draws below stay inside these ranges and needn't reach their ends.
There are 2 independent parts, one for each index of `grp`. The reference program is written for one: setup_inputs(seed, part) draws one part's arguments, and reference() takes and returns one part's arrays. A program takes and returns all parts, laid end to end along the dimension named above; an argument that names none is the same for every part. Nothing has to cross between parts.
Inputs may be any that keep to these rules, and one draw needn't show every extreme that they name: `tile_table`: each pair of input blocks (p, q) with p <= q < 8 stands in exactly one row, as [p, q].
All inputs are finite; a program needn't handle non-finite values.
Results may differ from the reference program's by a relative error of at most 0.0057.
Values may be sent and summed in bfloat16 or wider, within the bound.
No kernel may reach another device: no remote copies, remote signals or barrier semaphores. Data moves between devices by JAX's collectives and lax.ppermute only.
A program may use at most 192 MiB of HBM per device.

```python
import jax
import jax.numpy as jnp
import numpy as np
from jax import lax

INPUTS = 2048
NFFT = 2048
TAPS = 4
CHAN = 64
TILE = 256
TIMES = 8
SAMPLES = 16384
NB = 8
NTILES = 36


def draw_tile_table(key, part):
    key = jax.random.fold_in(key, 7)
    pairs = np.array([[first_block, second_block] for first_block in range(NB) for second_block in range(first_block, NB)], dtype=np.int32)
    order = jax.random.permutation(key, NTILES)
    return jnp.asarray(pairs, dtype=jnp.int32)[order]


def levels(key, extent, shards, low, top_value):
    level = 1.0
    for position, parts in shards:
        steps = jax.random.uniform(jax.random.fold_in(jax.random.fold_in(key, 6), position), (parts,), jnp.float32, low / len(shards), top_value / len(shards))
        level = level * jnp.repeat(jnp.exp(steps), extent[position] // parts).reshape((-1,) + (1,) * (len(extent) - 1 - position))
    return level


def gaussian(key, shape, scale, most, shards=(), held_as=jnp.bfloat16):
    loudness = levels(key, shape, shards, -0.22, 0.18) if shards else 1.0
    result = jax.random.normal(key, shape, jnp.float32) * scale * loudness
    return jnp.minimum(jnp.maximum(result, -most), most).astype(held_as)


def setup_inputs(seed: int = 0, part: int = 0) -> dict:
    key_of = jax.random.split(jax.random.key(seed), 4)
    part_splits = jax.random.split(jax.random.fold_in(key_of[3], part), 4)
    return {
        "raw_samples": gaussian(part_splits[0], (INPUTS, SAMPLES), 4.0, 24.0, ((0, 2), (1, 8))),
        "pfb_window": gaussian(key_of[1], (TAPS, NFFT), 0.12, 0.75, (), jnp.float32),
        "tile_table": draw_tile_table(jax.random.fold_in(key_of[3], 71), part),
    }


def channel_basis():
    sample_index = jnp.arange(NFFT, dtype=jnp.int32)
    channel_index = CHAN + jnp.arange(CHAN, dtype=jnp.int32)
    wrapped = sample_index[:, None] * channel_index[None, :] % NFFT
    phase_angle = wrapped.astype(jnp.float32) * (2.0 * jnp.pi / NFFT)
    scale = 1.0 / jnp.sqrt(jnp.float32(NFFT))
    return jnp.concatenate([jnp.cos(phase_angle), -jnp.sin(phase_angle)], axis=1) * scale

def reference(raw_samples, pfb_window, tile_table):
    cosine_table = channel_basis()

    def frame_spectrum(frame_index):
        running = jnp.zeros((INPUTS, NFFT), jnp.float32)
        for tap_lag in range(TAPS):
            source = frame_index - tap_lag
            first_column = (jnp.maximum(source, 0) * NFFT).astype(jnp.int32)
            raw_piece = lax.dynamic_slice_in_dim(raw_samples, first_column, NFFT, 1).astype(jnp.float32)
            running = running + jnp.where(source >= 0, pfb_window[tap_lag][None, :] * raw_piece, 0.0)
        spectrum = jnp.dot(running, cosine_table, precision=lax.Precision.HIGHEST)
        return spectrum.T.reshape(2, CHAN, INPUTS).astype(jnp.bfloat16)
    spectra = lax.map(frame_spectrum, jnp.arange(TIMES, dtype=jnp.int32))
    tile_rows = tile_table[:, 0]
    tile_cols = tile_table[:, 1]

    def channel_power(channel_data):
        blocks = channel_data.reshape(TIMES, 2, NB, TILE).astype(jnp.float32)
        left_blocks = jnp.take(blocks, tile_rows, axis=2)
        right_blocks = jnp.take(blocks, tile_cols, axis=2)
        left_real = left_blocks[:, 0]
        left_imag = left_blocks[:, 1]
        stacked_left = jnp.concatenate([left_real, left_imag], axis=0)
        rotated = jnp.concatenate([left_imag, -left_real], axis=0)
        combined = jnp.concatenate([stacked_left, rotated], axis=2)
        stacked_right = jnp.concatenate([right_blocks[:, 0], right_blocks[:, 1]], axis=0)
        products = jnp.einsum('stu,stv->tuv', combined, stacked_right)
        products = products.reshape(NTILES, 2, TILE, TILE) * (1.0 / TIMES)
        return products.astype(jnp.bfloat16)
    return lax.map(channel_power, jnp.transpose(spectra, (2, 0, 1, 3)))
```

```python
import functools

import jax
import jax.numpy as jnp
import numpy as np
from jax import lax
from jax.experimental import pallas as pl
from jax.experimental.pallas import tpu as pltpu
from jax.sharding import PartitionSpec as P

INPUTS = 2048
NFFT = 2048
TAPS = 4
CHAN = 64
TILE = 256
NB = INPUTS // TILE

CHUNKS = 1


def basis_rows(owners, first, count):
    per_owner = CHAN // owners
    chan = np.arange(owners)[:, None] * per_owner + first + np.arange(count)[None, :]
    wrapped = (np.arange(NFFT, dtype=np.int64)[None, :] * (CHAN + chan.reshape(-1, 1))) % NFFT
    angle = wrapped.astype(np.float64) * (2.0 * np.pi / NFFT)
    both = np.stack([np.cos(angle), -np.sin(angle)], axis=1) / np.sqrt(NFFT)
    return both.reshape(-1, NFFT).astype(np.float32)


def tap_sum(owners, count):
    matrix = np.zeros((count, 2, owners, owners, TAPS, count, 2), np.float32)
    for frame in range(owners):
        for tap in range(min(TAPS, frame + 1)):
            for chan in range(count):
                for part in range(2):
                    matrix[chan, part, frame, frame - tap, tap, chan, part] = 1.0
    return matrix.reshape(count * 2 * owners, -1)


def left_factors(owners, count):
    depth = count * 2 * owners
    real = np.zeros((count, 2, owners, count, 2, owners), np.float32)
    imag = np.zeros((count, 2, owners, count, 2, owners), np.float32)
    for chan in range(count):
        for frame in range(owners):
            real[chan, 0, frame, chan, 0, frame] = 1.0 / owners
            real[chan, 1, frame, chan, 1, frame] = 1.0 / owners
            imag[chan, 1, frame, chan, 0, frame] = 1.0 / owners
            imag[chan, 0, frame, chan, 1, frame] = -1.0 / owners
    return np.stack([real.reshape(depth, depth), imag.reshape(depth, depth)])


def transform_kernel(group, basis_ref, window_ref, samples_ref, out_ref, high, low):
    @pl.when(pl.program_id(0) == 0)
    def _():
        for first in range(0, basis_ref.shape[0], group):
            basis = basis_ref[first : first + group, :]
            weights = jnp.concatenate([basis * window_ref[k : k + 1, :] for k in range(TAPS)], axis=0)
            rounded = weights.astype(jnp.bfloat16)
            rows = pl.ds(first * TAPS, group * TAPS)
            high[rows, :] = rounded
            low[rows, :] = (weights - rounded.astype(jnp.float32)).astype(jnp.bfloat16)

    contract = (((1,), (1,)), ((), ()))
    samples = samples_ref[...]
    total = lax.dot_general(high[...], samples, contract, preferred_element_type=jnp.float32)
    total += lax.dot_general(low[...], samples, contract, preferred_element_type=jnp.float32)
    out_ref[...] = total.astype(out_ref.dtype)


def transform(samples, window, owners, first, count):
    inputs = samples.shape[0]
    basis = basis_rows(owners, first, count)
    rows = basis.shape[0]
    cols = 2 * count
    together = 1 if cols % 8 == 0 else 8 // cols
    group = cols * together
    block = 256
    out = pl.pallas_call(
        functools.partial(transform_kernel, group),
        grid=(inputs // block,),
        in_specs=[
            pl.BlockSpec((rows, NFFT), lambda i: (0, 0)),
            pl.BlockSpec((TAPS, NFFT), lambda i: (0, 0)),
            pl.BlockSpec((block, NFFT), lambda i: (i, 0)),
        ],
        out_specs=pl.BlockSpec((rows * TAPS, block), lambda i: (0, i)),
        out_shape=jax.ShapeDtypeStruct((rows * TAPS, inputs), jnp.bfloat16),
        scratch_shapes=[pltpu.VMEM((rows * TAPS, NFFT), jnp.bfloat16)] * 2,
        compiler_params=pltpu.CompilerParams(vmem_limit_bytes=48 << 20),
    )(jnp.asarray(basis), window, samples)
    if together > 1:
        out = out.reshape(owners // together, TAPS, together, cols, inputs)
        out = jnp.transpose(out, (0, 2, 1, 3, 4))
    return out.reshape(owners, TAPS * cols, inputs)


def power_kernel(count, table_ref, where_ref, own_ref, other_ref, left_ref, out_ref, left, right):
    depth = own_ref.shape[0]
    half = NB // 2

    @pl.when(pl.program_id(0) == 0)
    def _():
        chan = lax.broadcasted_iota(jnp.int32, (depth, TILE), 0) // (depth // count)
        for index in range(NB):
            ref = own_ref if index < half else other_ref
            base = where_ref[0] if index < half else half - where_ref[0]
            place = base + index % half
            piece = ref[:, (index % half) * TILE : (index % half + 1) * TILE]
            for part in range(2):
                turned = lax.dot_general(
                    piece, left_ref[part], (((0,), (0,)), ((), ())), preferred_element_type=jnp.float32
                )
                left[place, part * TILE : (part + 1) * TILE, :] = turned.astype(jnp.bfloat16)
            for c in range(count):
                right[place, c] = jnp.where(chan == c, piece, jnp.zeros_like(piece))

    j = pl.program_id(0)
    first = left[table_ref[j, 0]]
    q = table_ref[j, 1]
    for c in range(count):
        power = jnp.dot(first, right[q, c], preferred_element_type=jnp.float32)
        out_ref[c, 0] = power.astype(jnp.bfloat16).reshape(2, TILE, TILE)


def cross_power(table, where, own, other, count, total, chunk, previous):
    depth, width = own.shape
    tiles = table.shape[0]
    owners = depth // (2 * count)
    whole = lambda j, *_: (0, 0)
    in_specs = [
        pl.BlockSpec((depth, width), whole),
        pl.BlockSpec((depth, width), whole),
        pl.BlockSpec((2, depth, depth), lambda j, *_: (0, 0, 0)),
    ]
    args = [table, where, own, other, jnp.asarray(left_factors(owners, count), jnp.bfloat16)]
    kernel = functools.partial(power_kernel, count)
    aliases = {}
    if previous is not None:
        in_specs.append(pl.BlockSpec(memory_space=pl.ANY))
        args.append(previous)
        aliases = {5: 0}
        inner = kernel
        kernel = lambda t, w, a, b, l, _, o, left, right: inner(t, w, a, b, l, o, left, right)
    return pl.pallas_call(
        kernel,
        grid_spec=pltpu.PrefetchScalarGridSpec(
            num_scalar_prefetch=2,
            grid=(tiles,),
            in_specs=in_specs,
            out_specs=pl.BlockSpec((count, 1, 2, TILE, TILE), lambda j, *_: (chunk, j, 0, 0, 0)),
            scratch_shapes=[
                pltpu.VMEM((NB, 2 * TILE, depth), jnp.bfloat16),
                pltpu.VMEM((NB, count, depth, TILE), jnp.bfloat16),
            ],
        ),
        out_shape=jax.ShapeDtypeStruct((total, tiles, 2, TILE, TILE), jnp.bfloat16),
        input_output_aliases=aliases,
        compiler_params=pltpu.CompilerParams(vmem_limit_bytes=48 << 20),
    )(*args)


def local(raw_samples, pfb_window, tile_table):
    owners = lax.axis_size("tm")
    inputs = raw_samples.shape[0]
    total = CHAN // owners
    chunks = CHUNKS if total % CHUNKS == 0 else 1
    count = total // chunks
    where = (lax.axis_index("inp") * (NB // 2)).astype(jnp.int32).reshape(1)
    turned = []
    for chunk in range(chunks):
        partial = transform(raw_samples, pfb_window, owners, chunk * count, count)
        turned.append(lax.all_to_all(partial, "tm", split_axis=0, concat_axis=0, tiled=True))
    out = None
    for chunk in range(chunks):
        add = jnp.asarray(tap_sum(owners, count), jnp.bfloat16)
        own = jnp.dot(add, turned[chunk].reshape(-1, inputs), preferred_element_type=jnp.float32)
        own = own.astype(jnp.bfloat16)
        other = lax.ppermute(own, "inp", [(0, 1), (1, 0)])
        out = cross_power(tile_table, where, own, other, count, total, chunk, out)
    return out


def solution(mesh):
    return jax.shard_map(
        local,
        mesh=mesh,
        in_specs=(P(("grp", "inp"), "tm"), P(), P("inp", None)),
        out_specs=P(("grp", "tm"), "inp", None, None, None),
        check_vma=False,
    )
```

```python
import functools

import jax
import jax.numpy as jnp
import numpy as np
from jax import lax
from jax.experimental import pallas as pl
from jax.experimental.pallas import tpu as pltpu
from jax.sharding import PartitionSpec as P

INPUTS = 2048
NFFT = 2048
TAPS = 4
CHAN = 64
TILE = 256
NB = INPUTS // TILE
HALF = NB // 2


def params(mib):
    return pltpu.CompilerParams(vmem_limit_bytes=mib << 20)


def cost(flops, moved):
    return pl.CostEstimate(flops=flops, transcendentals=0, bytes_accessed=moved)


def basis_rows(owners, first, count):
    per_owner = CHAN // owners
    chan = np.arange(owners)[:, None] * per_owner + first + np.arange(count)[None, :]
    wrapped = (np.arange(NFFT, dtype=np.int64)[None, :] * (CHAN + chan.reshape(-1, 1))) % NFFT
    angle = wrapped.astype(np.float64) * (2.0 * np.pi / NFFT)
    both = np.stack([np.cos(angle), -np.sin(angle)], axis=1) / np.sqrt(NFFT)
    return both.reshape(-1, NFFT).astype(np.float32)


def transform_kernel(group, segments, basis_hbm, window_hbm, samples_hbm, *refs):
    *out_refs, basis, window, samples, high, low, sems = refs
    blocks = 2
    size = samples.shape[0] // blocks
    copies = [
        pltpu.make_async_copy(basis_hbm, basis, sems.at[0]),
        pltpu.make_async_copy(window_hbm, window, sems.at[1]),
    ]
    for b in range(blocks):
        rows = pl.ds(b * size, size)
        copies.append(pltpu.make_async_copy(samples_hbm.at[rows], samples.at[rows], sems.at[2 + b]))
    for copy in copies:
        copy.start()
    copies[0].wait()
    copies[1].wait()
    for index, (chunk, distance) in enumerate(segments):
        place = distance
        if len(out_refs) > 1:
            place = lax.bitwise_xor(lax.axis_index("tm"), distance)
        rows = basis[chunk, pl.ds(pl.multiple_of(place * group, group), group), :]
        weights = jnp.concatenate([rows * window[k : k + 1, :] for k in range(TAPS)], axis=0)
        rounded = weights.astype(jnp.bfloat16)
        where = pl.ds(index * group * TAPS, group * TAPS)
        high[where, :] = rounded
        low[where, :] = (weights - rounded.astype(jnp.float32)).astype(jnp.bfloat16)

    contract = (((1,), (1,)), ((), ()))
    for b in range(blocks):
        copies[2 + b].wait()
        piece = samples[b * size : (b + 1) * size, :]
        total = lax.dot_general(high[...], piece, contract, preferred_element_type=jnp.float32)
        total += lax.dot_general(low[...], piece, contract, preferred_element_type=jnp.float32)
        total = total.astype(jnp.bfloat16)
        first = 0
        for out_ref in out_refs:
            out_ref[:, b * size : (b + 1) * size] = total[first : first + out_ref.shape[0]]
            first += out_ref.shape[0]


def transform(samples, window, owners, chunks, count, group, segments, outs):
    inputs = samples.shape[0]
    basis = np.stack([basis_rows(owners, chunk * count, count) for chunk in range(chunks)])
    rows = len(segments) * group * TAPS
    hbm = pl.BlockSpec(memory_space=pl.ANY)
    return pl.pallas_call(
        functools.partial(transform_kernel, group, segments),
        in_specs=[hbm] * 3,
        out_specs=[pl.BlockSpec(memory_space=pltpu.VMEM)] * len(outs),
        out_shape=[jax.ShapeDtypeStruct((n * group * TAPS, inputs), jnp.bfloat16) for n in outs],
        scratch_shapes=[
            pltpu.VMEM(basis.shape, jnp.float32),
            pltpu.VMEM((TAPS, NFFT), jnp.float32),
            pltpu.VMEM((inputs, NFFT), jnp.bfloat16),
            pltpu.VMEM((rows, NFFT), jnp.bfloat16),
            pltpu.VMEM((rows, NFFT), jnp.bfloat16),
            pltpu.SemaphoreType.DMA((4,)),
        ],
        compiler_params=params(60),
        cost_estimate=cost(4 * rows * inputs * NFFT, 8 << 20),
    )(jnp.asarray(basis), window, samples)


def tap_matrix(frames, pieces, count, first):
    cols = 2 * count
    shape = (cols * frames, pieces * TAPS * cols)
    row = lax.broadcasted_iota(jnp.int32, shape, 0)
    col = lax.broadcasted_iota(jnp.int32, shape, 1)
    source = lax.bitwise_xor(col // (TAPS * cols), first)
    hit = (col % cols == row // frames) & (row % frames - (col // cols) % TAPS == source)
    return jnp.where(hit, 1.0, 0.0).astype(jnp.bfloat16)


def tap_sum_kernel(owners, count, spectra_ref, out_ref):
    add = tap_matrix(owners, owners, count, 0)
    out_ref[...] = jnp.dot(add, spectra_ref[...], preferred_element_type=jnp.float32).astype(jnp.bfloat16)


def near_sum_kernel(owners, count, *refs):
    *parts, near_first, near_second, facing = refs
    depth = TAPS * 2 * count
    add = tap_matrix(owners, owners // 2, count, lax.axis_index("tm"))
    for index, out_ref in enumerate((near_first, near_second, facing)):
        spectra = jnp.concatenate([ref[index * depth : (index + 1) * depth, :] for ref in parts], axis=0)
        total = jnp.dot(add, spectra, preferred_element_type=jnp.float32)
        out_ref[...] = total.astype(out_ref.dtype)


def far_sum_kernel(owners, count, near_ref, *refs):
    *parts, out_ref = refs
    half = owners // 2
    add = tap_matrix(owners, half, count, lax.bitwise_xor(lax.axis_index("tm"), half))
    spectra = jnp.concatenate([ref[...] for ref in parts], axis=0)
    total = near_ref[...] + jnp.dot(add, spectra, preferred_element_type=jnp.float32)
    out_ref[...] = total.astype(jnp.bfloat16)


def join_kernel(near_ref, far_ref, out_ref):
    out_ref[...] = (near_ref[...] + far_ref[...].astype(jnp.float32)).astype(jnp.bfloat16)


def small(kernel, outs, inputs):
    vmem = pl.BlockSpec(memory_space=pltpu.VMEM)
    return pl.pallas_call(
        kernel,
        in_specs=[vmem] * len(inputs),
        out_specs=[vmem] * len(outs),
        out_shape=outs,
        compiler_params=params(16),
        cost_estimate=cost(1 << 28, 1 << 20),
    )(*inputs)


def power_kernel(count, chunk, together, table_ref, own_ref, other_ref, *refs):
    out_ref, left, right, buf, sem = refs[-5:]
    depth = own_ref.shape[0]
    frames = depth // (2 * count)
    slots = buf.shape[0]
    steps = out_ref.shape[1] // together
    mine = lax.axis_index("inp") * HALF

    row = lax.broadcasted_iota(jnp.int32, (depth, depth), 0)
    col = lax.broadcasted_iota(jnp.int32, (depth, depth), 1)
    scale = 1.0 / frames
    real = jnp.where(row == col, scale, 0.0).astype(jnp.bfloat16)
    sign = jnp.where((col // frames) % 2 == 0, scale, -scale)
    partner = (row // (2 * frames) == col // (2 * frames)) & (row % frames == col % frames)
    imag = jnp.where(partner & (row != col), sign, 0.0).astype(jnp.bfloat16)
    chan = lax.broadcasted_iota(jnp.int32, (depth, TILE), 0) // (2 * frames)
    for index in range(NB):
        ref = own_ref if index < HALF else other_ref
        place = (mine if index < HALF else HALF - mine) + index % HALF
        piece = ref[:, (index % HALF) * TILE : (index % HALF + 1) * TILE]
        for part, turn in enumerate((real, imag)):
            turned = lax.dot_general(piece, turn, (((0,), (0,)), ((), ())), preferred_element_type=jnp.float32)
            left[place, part * TILE : (part + 1) * TILE, :] = turned.astype(jnp.bfloat16)
        for c in range(count):
            right[place, c] = jnp.where(chan == c, piece, jnp.zeros_like(piece))

    def copy(step):
        slot = lax.rem(step, slots)
        where = out_ref.at[pl.ds(chunk * count, count), pl.ds(step * together, together)]
        return pltpu.make_async_copy(buf.at[slot], where, sem.at[slot])

    def body(step, carry):
        slot = lax.rem(step, slots)

        @pl.when(step >= slots)
        def _():
            copy(step - slots).wait()

        for u in range(together):
            p = table_ref[step * together + u, 0]
            q = table_ref[step * together + u, 1]
            for c in range(count):
                for part in range(2):
                    first = left[p, part * TILE : (part + 1) * TILE, :]
                    power = jnp.dot(first, right[q, c], preferred_element_type=jnp.float32)
                    buf[slot, c, u, part] = power.astype(jnp.bfloat16)
        copy(step).start()
        return carry

    lax.fori_loop(0, steps, body, 0)

    def drain(step, carry):
        copy(step).wait()
        return carry

    lax.fori_loop(steps - slots, steps, drain, 0)


def cross_power(table, own, other, count, total, chunk, previous):
    depth, width = own.shape
    tiles = table.shape[0]
    together = 2 if tiles % 2 == 0 else 1
    vmem = pl.BlockSpec(memory_space=pltpu.VMEM)
    hbm = pl.BlockSpec(memory_space=pl.ANY)
    in_specs = [pl.BlockSpec(memory_space=pltpu.SMEM), vmem, vmem]
    args = [table, own, other]
    aliases = {}
    if previous is not None:
        in_specs.append(hbm)
        args.append(previous)
        aliases = {3: 0}
    return pl.pallas_call(
        functools.partial(power_kernel, count, chunk, together),
        in_specs=in_specs,
        out_specs=hbm,
        out_shape=jax.ShapeDtypeStruct((total, tiles, 2, TILE, TILE), jnp.bfloat16),
        scratch_shapes=[
            pltpu.VMEM((NB, 2 * TILE, depth), jnp.bfloat16),
            pltpu.VMEM((NB, count, depth, TILE), jnp.bfloat16),
            pltpu.VMEM((3, count, together, 2, TILE, TILE), jnp.bfloat16),
            pltpu.SemaphoreType.DMA((3,)),
        ],
        input_output_aliases=aliases,
        compiler_params=params(24),
        cost_estimate=cost(2 * tiles * count * 2 * TILE * TILE * 256, tiles * count * 4 * TILE * TILE),
    )(*args)


def finish(table, own, count, total, chunk, out):
    other = lax.ppermute(own, "inp", [(0, 1), (1, 0)])
    return cross_power(table, own, other, count, total, chunk, out)


def turn_whole(samples, window, table, owners, total):
    inputs = samples.shape[0]
    cols = 2 * total
    together = 1 if cols % 8 == 0 else 8 // cols
    group = cols * together
    segments = [(0, d) for d in range(owners // together)]
    (partial,) = transform(samples, window, owners, 1, total, group, segments, [len(segments)])
    partial = partial.reshape(owners // together, TAPS, together, cols, inputs)
    partial = jnp.transpose(partial, (0, 2, 1, 3, 4)).reshape(owners, TAPS * cols, inputs)
    turned = lax.all_to_all(partial, "tm", split_axis=0, concat_axis=0, tiled=True)
    kernel = functools.partial(tap_sum_kernel, owners, total)
    sums = jax.ShapeDtypeStruct((cols * owners, inputs), jnp.bfloat16)
    (own,) = small(kernel, [sums], [turned.reshape(-1, inputs)])
    return finish(table, own, total, total, 0, None)


def local(raw_samples, pfb_window, tile_table):
    owners = lax.axis_size("tm")
    total = CHAN // owners
    if owners != 8:
        return turn_whole(raw_samples, pfb_window, tile_table, owners, total)

    inputs = raw_samples.shape[0]
    count = total // 2
    half = owners // 2
    segments = [(0, half + d) for d in range(half)]
    for d in range(half):
        segments += [(0, d), (1, d), (1, half + d)]
    outs = [1] * half + [3] * half
    sent = transform(raw_samples, pfb_window, owners, 2, count, 2 * count, segments, outs)

    def swap(block, d):
        return block if d == 0 else lax.ppermute(block, "tm", [(i, i ^ d) for i in range(owners)])

    far = [swap(sent[d], half + d) for d in range(half)]
    near = [swap(sent[half + d], d) for d in range(half)]
    exact = jax.ShapeDtypeStruct((2 * count * owners, inputs), jnp.float32)
    rounded = jax.ShapeDtypeStruct((2 * count * owners, inputs), jnp.bfloat16)
    kernel = functools.partial(near_sum_kernel, owners, count)
    near_first, near_second, facing = small(kernel, [exact, exact, rounded], near)
    faced = swap(facing, half)
    kernel = functools.partial(far_sum_kernel, owners, count)
    (own,) = small(kernel, [rounded], [near_first] + far)
    out = finish(tile_table, own, count, total, 0, None)
    faced, out = lax.optimization_barrier((faced, out))
    (own,) = small(join_kernel, [rounded], [near_second, faced])
    return finish(tile_table, own, count, total, 1, out)


def solution(mesh):
    return jax.shard_map(
        local,
        mesh=mesh,
        in_specs=(P(("grp", "inp"), "tm"), P(), P("inp", None)),
        out_specs=P(("grp", "tm"), "inp", None, None, None),
        check_vma=False,
    )
```

```python
import functools

import jax
import jax.numpy as jnp
import numpy as np
from jax import lax
from jax.experimental import pallas as pl
from jax.experimental.pallas import tpu as pltpu
from jax.sharding import PartitionSpec as P

INPUTS = 2048
NFFT = 2048
TAPS = 4
CHAN = 64
TILE = 256
NB = INPUTS // TILE
HALF = NB // 2


def params(mib):
    return pltpu.CompilerParams(vmem_limit_bytes=mib << 20)


def cost(flops, moved):
    return pl.CostEstimate(flops=flops, transcendentals=0, bytes_accessed=moved)


def basis_rows(owners, first, count):
    per_owner = CHAN // owners
    chan = np.arange(owners)[:, None] * per_owner + first + np.arange(count)[None, :]
    wrapped = (np.arange(NFFT, dtype=np.int64)[None, :] * (CHAN + chan.reshape(-1, 1))) % NFFT
    angle = wrapped.astype(np.float64) * (2.0 * np.pi / NFFT)
    both = np.stack([np.cos(angle), -np.sin(angle)], axis=1) / np.sqrt(NFFT)
    return both.reshape(-1, NFFT).astype(np.float32)


def transform_kernel(group, segments, basis_hbm, window_hbm, samples_hbm, *refs):
    *out_refs, basis, window, samples, high, low, sems = refs
    blocks = 2
    size = samples.shape[0] // blocks
    copies = [
        pltpu.make_async_copy(basis_hbm, basis, sems.at[0]),
        pltpu.make_async_copy(window_hbm, window, sems.at[1]),
    ]
    for b in range(blocks):
        rows = pl.ds(b * size, size)
        copies.append(pltpu.make_async_copy(samples_hbm.at[rows], samples.at[rows], sems.at[2 + b]))
    for copy in copies:
        copy.start()
    copies[0].wait()
    copies[1].wait()
    for index, (chunk, distance) in enumerate(segments):
        place = distance
        if len(out_refs) > 1:
            place = lax.bitwise_xor(lax.axis_index("tm"), distance)
        rows = basis[chunk, pl.ds(pl.multiple_of(place * group, group), group), :]
        weights = jnp.concatenate([rows * window[k : k + 1, :] for k in range(TAPS)], axis=0)
        rounded = weights.astype(jnp.bfloat16)
        where = pl.ds(index * group * TAPS, group * TAPS)
        high[where, :] = rounded
        low[where, :] = (weights - rounded.astype(jnp.float32)).astype(jnp.bfloat16)

    contract = (((1,), (1,)), ((), ()))
    for b in range(blocks):
        copies[2 + b].wait()
        piece = samples[b * size : (b + 1) * size, :]
        total = lax.dot_general(high[...], piece, contract, preferred_element_type=jnp.float32)
        total += lax.dot_general(low[...], piece, contract, preferred_element_type=jnp.float32)
        total = total.astype(jnp.bfloat16)
        first = 0
        for out_ref in out_refs:
            out_ref[:, b * size : (b + 1) * size] = total[first : first + out_ref.shape[0]]
            first += out_ref.shape[0]


def transform(samples, window, owners, chunks, count, group, segments, outs):
    inputs = samples.shape[0]
    basis = np.stack([basis_rows(owners, chunk * count, count) for chunk in range(chunks)])
    rows = len(segments) * group * TAPS
    hbm = pl.BlockSpec(memory_space=pl.ANY)
    return pl.pallas_call(
        functools.partial(transform_kernel, group, segments),
        in_specs=[hbm] * 3,
        out_specs=[pl.BlockSpec(memory_space=pltpu.VMEM)] * len(outs),
        out_shape=[jax.ShapeDtypeStruct((n * group * TAPS, inputs), jnp.bfloat16) for n in outs],
        scratch_shapes=[
            pltpu.VMEM(basis.shape, jnp.float32),
            pltpu.VMEM((TAPS, NFFT), jnp.float32),
            pltpu.VMEM((inputs, NFFT), jnp.bfloat16),
            pltpu.VMEM((rows, NFFT), jnp.bfloat16),
            pltpu.VMEM((rows, NFFT), jnp.bfloat16),
            pltpu.SemaphoreType.DMA((4,)),
        ],
        compiler_params=params(40),
        cost_estimate=cost(4 * rows * inputs * NFFT, 8 << 20),
    )(*[pltpu.with_memory_space_constraint(a, pltpu.HBM) for a in (jnp.asarray(basis), window, samples)])


def tap_matrix(frames, pieces, count, first):
    cols = 2 * count
    shape = (cols * frames, pieces * TAPS * cols)
    row = lax.broadcasted_iota(jnp.int32, shape, 0)
    col = lax.broadcasted_iota(jnp.int32, shape, 1)
    source = lax.bitwise_xor(col // (TAPS * cols), first)
    hit = (col % cols == row // frames) & (row % frames - (col // cols) % TAPS == source)
    return jnp.where(hit, 1.0, 0.0).astype(jnp.bfloat16)


def tap_sum_kernel(owners, count, spectra_ref, out_ref):
    add = tap_matrix(owners, owners, count, 0)
    out_ref[...] = jnp.dot(add, spectra_ref[...], preferred_element_type=jnp.float32).astype(jnp.bfloat16)


def near_sum_kernel(owners, count, *refs):
    *parts, near_first, near_second, facing = refs
    depth = TAPS * 2 * count
    add = tap_matrix(owners, owners // 2, count, lax.axis_index("tm"))
    for index, out_ref in enumerate((near_first, near_second, facing)):
        spectra = jnp.concatenate([ref[index * depth : (index + 1) * depth, :] for ref in parts], axis=0)
        total = jnp.dot(add, spectra, preferred_element_type=jnp.float32)
        out_ref[...] = total.astype(out_ref.dtype)


def far_sum_kernel(owners, count, near_ref, *refs):
    *parts, out_ref = refs
    half = owners // 2
    add = tap_matrix(owners, half, count, lax.bitwise_xor(lax.axis_index("tm"), half))
    spectra = jnp.concatenate([ref[...] for ref in parts], axis=0)
    total = near_ref[...] + jnp.dot(add, spectra, preferred_element_type=jnp.float32)
    out_ref[...] = total.astype(jnp.bfloat16)


def join_kernel(near_ref, far_ref, out_ref):
    out_ref[...] = (near_ref[...] + far_ref[...].astype(jnp.float32)).astype(jnp.bfloat16)


def small(kernel, outs, inputs):
    vmem = pl.BlockSpec(memory_space=pltpu.VMEM)
    return pl.pallas_call(
        kernel,
        in_specs=[vmem] * len(inputs),
        out_specs=[vmem] * len(outs),
        out_shape=outs,
        compiler_params=params(16),
        cost_estimate=cost(1 << 28, 1 << 20),
    )(*inputs)


def power_kernel(count, chunk, together, table_ref, own_ref, other_ref, *refs):
    out_ref, left, right, buf, sem = refs[-5:]
    depth = own_ref.shape[0]
    frames = depth // (2 * count)
    slots = buf.shape[0]
    steps = out_ref.shape[1] // together
    mine = lax.axis_index("inp") * HALF

    row = lax.broadcasted_iota(jnp.int32, (depth, depth), 0)
    col = lax.broadcasted_iota(jnp.int32, (depth, depth), 1)
    scale = 1.0 / frames
    real = jnp.where(row == col, scale, 0.0).astype(jnp.bfloat16)
    sign = jnp.where((col // frames) % 2 == 0, scale, -scale)
    partner = (row // (2 * frames) == col // (2 * frames)) & (row % frames == col % frames)
    imag = jnp.where(partner & (row != col), sign, 0.0).astype(jnp.bfloat16)
    chan = lax.broadcasted_iota(jnp.int32, (depth, TILE), 0) // (2 * frames)
    for index in range(NB):
        ref = own_ref if index < HALF else other_ref
        place = (mine if index < HALF else HALF - mine) + index % HALF
        piece = ref[:, (index % HALF) * TILE : (index % HALF + 1) * TILE]
        for part, turn in enumerate((real, imag)):
            turned = lax.dot_general(piece, turn, (((0,), (0,)), ((), ())), preferred_element_type=jnp.float32)
            left[place, part * TILE : (part + 1) * TILE, :] = turned.astype(jnp.bfloat16)
        for c in range(count):
            right[place, c] = jnp.where(chan == c, piece, jnp.zeros_like(piece))

    def copies(step):
        slot = lax.rem(step, slots)
        tiles = pl.ds(step * together, together)
        return [
            pltpu.make_async_copy(buf.at[slot, c], out_ref.at[chunk * count + c, tiles], sem.at[slot, c])
            for c in range(count)
        ]

    def body(step, carry):
        slot = lax.rem(step, slots)

        @pl.when(step >= slots)
        def _():
            for done in copies(step - slots):
                done.wait()

        pairs = [(table_ref[step * together + u, 0], table_ref[step * together + u, 1]) for u in range(together)]
        for c, ready in enumerate(copies(step)):
            for u, (p, q) in enumerate(pairs):
                for part in range(2):
                    first = left[p, part * TILE : (part + 1) * TILE, :]
                    power = jnp.dot(first, right[q, c], preferred_element_type=jnp.float32)
                    buf[slot, c, u, part] = power.astype(jnp.bfloat16)
            ready.start()
        return carry

    lax.fori_loop(0, steps, body, 0)

    def drain(step, carry):
        for done in copies(step):
            done.wait()
        return carry

    lax.fori_loop(steps - slots, steps, drain, 0)


def cross_power(table, own, other, count, total, chunk, previous):
    depth, width = own.shape
    tiles = table.shape[0]
    together = 3 if tiles % 3 == 0 else 1
    vmem = pl.BlockSpec(memory_space=pltpu.VMEM)
    hbm = pl.BlockSpec(memory_space=pl.ANY)
    in_specs = [pl.BlockSpec(memory_space=pltpu.SMEM), vmem, vmem]
    args = [table, own, other]
    aliases = {}
    if previous is not None:
        in_specs.append(hbm)
        args.append(previous)
        aliases = {3: 0}
    return pl.pallas_call(
        functools.partial(power_kernel, count, chunk, together),
        in_specs=in_specs,
        out_specs=hbm,
        out_shape=jax.ShapeDtypeStruct((total, tiles, 2, TILE, TILE), jnp.bfloat16),
        scratch_shapes=[
            pltpu.VMEM((NB, 2 * TILE, depth), jnp.bfloat16),
            pltpu.VMEM((NB, count, depth, TILE), jnp.bfloat16),
            pltpu.VMEM((3, count, together, 2, TILE, TILE), jnp.bfloat16),
            pltpu.SemaphoreType.DMA((3, count)),
        ],
        input_output_aliases=aliases,
        compiler_params=params(32),
        cost_estimate=cost(2 * tiles * count * 2 * TILE * TILE * 256, tiles * count * 4 * TILE * TILE),
    )(*args)


def finish(table, own, count, total, chunk, out):
    other = lax.ppermute(own, "inp", [(0, 1), (1, 0)])
    return cross_power(table, own, other, count, total, chunk, out)


def turn_whole(samples, window, table, owners, total):
    inputs = samples.shape[0]
    cols = 2 * total
    together = 1 if cols % 8 == 0 else 8 // cols
    group = cols * together
    segments = [(0, d) for d in range(owners // together)]
    (partial,) = transform(samples, window, owners, 1, total, group, segments, [len(segments)])
    partial = partial.reshape(owners // together, TAPS, together, cols, inputs)
    partial = jnp.transpose(partial, (0, 2, 1, 3, 4)).reshape(owners, TAPS * cols, inputs)
    turned = lax.all_to_all(partial, "tm", split_axis=0, concat_axis=0, tiled=True)
    kernel = functools.partial(tap_sum_kernel, owners, total)
    sums = jax.ShapeDtypeStruct((cols * owners, inputs), jnp.bfloat16)
    (own,) = small(kernel, [sums], [turned.reshape(-1, inputs)])
    return finish(table, own, total, total, 0, None)


def local(raw_samples, pfb_window, tile_table):
    owners = lax.axis_size("tm")
    total = CHAN // owners
    if owners != 8:
        return turn_whole(raw_samples, pfb_window, tile_table, owners, total)

    inputs = raw_samples.shape[0]
    count = total // 2
    half = owners // 2
    segments = [(0, half + d) for d in range(half)]
    for d in range(half):
        segments += [(0, d), (1, d), (1, half + d)]
    outs = [1] * half + [3] * half
    sent = transform(raw_samples, pfb_window, owners, 2, count, 2 * count, segments, outs)

    def swap(block, d):
        return block if d == 0 else lax.ppermute(block, "tm", [(i, i ^ d) for i in range(owners)])

    far = [swap(sent[d], half + d) for d in range(half)]
    near = [swap(sent[half + d], d) for d in range(half)]
    exact = jax.ShapeDtypeStruct((2 * count * owners, inputs), jnp.float32)
    rounded = jax.ShapeDtypeStruct((2 * count * owners, inputs), jnp.bfloat16)
    kernel = functools.partial(near_sum_kernel, owners, count)
    near_first, near_second, facing = small(kernel, [exact, exact, rounded], near)
    faced = swap(facing, half)
    kernel = functools.partial(far_sum_kernel, owners, count)
    (own,) = small(kernel, [rounded], [near_first] + far)
    out = finish(tile_table, own, count, total, 0, None)
    faced, out = lax.optimization_barrier((faced, out))
    (own,) = small(join_kernel, [rounded], [near_second, faced])
    return finish(tile_table, own, count, total, 1, out)


def solution(mesh):
    return jax.shard_map(
        local,
        mesh=mesh,
        in_specs=(P(("grp", "inp"), "tm"), P(), P("inp", None)),
        out_specs=P(("grp", "tm"), "inp", None, None, None),
        check_vma=False,
    )
```

```python
import functools

import jax
import jax.numpy as jnp
import numpy as np
from jax import lax
from jax.experimental import pallas as pl
from jax.experimental.pallas import tpu as pltpu
from jax.sharding import PartitionSpec as P

INPUTS = 2048
NFFT = 2048
TAPS = 4
CHAN = 64
TILE = 256
NB = INPUTS // TILE
HALF = NB // 2


def params(mib):
    return pltpu.CompilerParams(vmem_limit_bytes=mib << 20)


def cost(flops, moved):
    return pl.CostEstimate(flops=flops, transcendentals=0, bytes_accessed=moved)


def basis_rows(owners, first, count):
    per_owner = CHAN // owners
    chan = np.arange(owners)[:, None] * per_owner + first + np.arange(count)[None, :]
    wrapped = (np.arange(NFFT, dtype=np.int64)[None, :] * (CHAN + chan.reshape(-1, 1))) % NFFT
    angle = wrapped.astype(np.float64) * (2.0 * np.pi / NFFT)
    both = np.stack([np.cos(angle), -np.sin(angle)], axis=1) / np.sqrt(NFFT)
    return both.reshape(-1, NFFT).astype(np.float32)


def transform_kernel(group, segments, basis_hbm, window_hbm, samples_hbm, *refs):
    *out_refs, basis, window, samples, high, sems = refs
    blocks = 2
    size = samples.shape[0] // blocks
    copies = [
        pltpu.make_async_copy(basis_hbm, basis, sems.at[0]),
        pltpu.make_async_copy(window_hbm, window, sems.at[1]),
    ]
    for b in range(blocks):
        rows = pl.ds(b * size, size)
        copies.append(pltpu.make_async_copy(samples_hbm.at[rows], samples.at[rows], sems.at[2 + b]))
    for copy in copies:
        copy.start()
    copies[0].wait()
    copies[1].wait()
    for index, (chunk, distance) in enumerate(segments):
        place = distance
        if len(out_refs) > 1:
            place = lax.bitwise_xor(lax.axis_index("tm"), distance)
        rows = basis[chunk, pl.ds(pl.multiple_of(place * group, group), group), :]
        weights = jnp.concatenate([rows * window[k : k + 1, :] for k in range(TAPS)], axis=0)
        high[pl.ds(index * group * TAPS, group * TAPS), :] = weights.astype(jnp.bfloat16)

    contract = (((1,), (1,)), ((), ()))
    for b in range(blocks):
        copies[2 + b].wait()
        piece = samples[b * size : (b + 1) * size, :]
        total = lax.dot_general(high[...], piece, contract, preferred_element_type=jnp.float32)
        total = total.astype(jnp.bfloat16)
        first = 0
        for out_ref in out_refs:
            out_ref[:, b * size : (b + 1) * size] = total[first : first + out_ref.shape[0]]
            first += out_ref.shape[0]


def transform(samples, window, owners, chunks, count, group, segments, outs):
    inputs = samples.shape[0]
    basis = np.stack([basis_rows(owners, chunk * count, count) for chunk in range(chunks)])
    rows = len(segments) * group * TAPS
    hbm = pl.BlockSpec(memory_space=pl.ANY)
    return pl.pallas_call(
        functools.partial(transform_kernel, group, segments),
        in_specs=[hbm] * 3,
        out_specs=[pl.BlockSpec(memory_space=pltpu.VMEM)] * len(outs),
        out_shape=[jax.ShapeDtypeStruct((n * group * TAPS, inputs), jnp.bfloat16) for n in outs],
        scratch_shapes=[
            pltpu.VMEM(basis.shape, jnp.float32),
            pltpu.VMEM((TAPS, NFFT), jnp.float32),
            pltpu.VMEM((inputs, NFFT), jnp.bfloat16),
            pltpu.VMEM((rows, NFFT), jnp.bfloat16),
            pltpu.SemaphoreType.DMA((4,)),
        ],
        compiler_params=params(40),
        cost_estimate=cost(4 * rows * inputs * NFFT, 8 << 20),
    )(*[pltpu.with_memory_space_constraint(a, pltpu.HBM) for a in (jnp.asarray(basis), window, samples)])


def tap_matrix(frames, pieces, count, first):
    cols = 2 * count
    shape = (cols * frames, pieces * TAPS * cols)
    row = lax.broadcasted_iota(jnp.int32, shape, 0)
    col = lax.broadcasted_iota(jnp.int32, shape, 1)
    source = lax.bitwise_xor(col // (TAPS * cols), first)
    hit = (col % cols == row // frames) & (row % frames - (col // cols) % TAPS == source)
    return jnp.where(hit, 1.0, 0.0).astype(jnp.bfloat16)


def tap_sum_kernel(owners, count, spectra_ref, out_ref):
    add = tap_matrix(owners, owners, count, 0)
    out_ref[...] = jnp.dot(add, spectra_ref[...], preferred_element_type=jnp.float32).astype(jnp.bfloat16)


def near_sum_kernel(owners, count, *refs):
    *parts, near_first, near_second, facing = refs
    depth = TAPS * 2 * count
    add = tap_matrix(owners, owners // 2, count, lax.axis_index("tm"))
    for index, out_ref in enumerate((near_first, near_second, facing)):
        spectra = jnp.concatenate([ref[index * depth : (index + 1) * depth, :] for ref in parts], axis=0)
        total = jnp.dot(add, spectra, preferred_element_type=jnp.float32)
        out_ref[...] = total.astype(out_ref.dtype)


def far_sum_kernel(owners, count, near_ref, *refs):
    *parts, out_ref = refs
    half = owners // 2
    add = tap_matrix(owners, half, count, lax.bitwise_xor(lax.axis_index("tm"), half))
    spectra = jnp.concatenate([ref[...] for ref in parts], axis=0)
    total = near_ref[...] + jnp.dot(add, spectra, preferred_element_type=jnp.float32)
    out_ref[...] = total.astype(jnp.bfloat16)


def join_kernel(near_ref, far_ref, out_ref):
    out_ref[...] = (near_ref[...] + far_ref[...].astype(jnp.float32)).astype(jnp.bfloat16)


def small(kernel, outs, inputs):
    vmem = pl.BlockSpec(memory_space=pltpu.VMEM)
    return pl.pallas_call(
        kernel,
        in_specs=[vmem] * len(inputs),
        out_specs=[vmem] * len(outs),
        out_shape=outs,
        compiler_params=params(16),
        cost_estimate=cost(1 << 28, 1 << 20),
    )(*inputs)


def power_kernel(count, chunk, together, table_ref, own_ref, other_ref, *refs):
    out_ref, left, right, buf, sem = refs[-5:]
    depth = own_ref.shape[0]
    frames = depth // (2 * count)
    slots = buf.shape[0]
    steps = out_ref.shape[1] // together
    mine = lax.axis_index("inp") * HALF

    row = lax.broadcasted_iota(jnp.int32, (depth, depth), 0)
    col = lax.broadcasted_iota(jnp.int32, (depth, depth), 1)
    scale = 1.0 / frames
    real = jnp.where(row == col, scale, 0.0).astype(jnp.bfloat16)
    sign = jnp.where((col // frames) % 2 == 0, scale, -scale)
    partner = (row // (2 * frames) == col // (2 * frames)) & (row % frames == col % frames)
    imag = jnp.where(partner & (row != col), sign, 0.0).astype(jnp.bfloat16)
    chan = lax.broadcasted_iota(jnp.int32, (depth, TILE), 0) // (2 * frames)
    for index in range(NB):
        ref = own_ref if index < HALF else other_ref
        place = (mine if index < HALF else HALF - mine) + index % HALF
        piece = ref[:, (index % HALF) * TILE : (index % HALF + 1) * TILE]
        for part, turn in enumerate((real, imag)):
            turned = lax.dot_general(piece, turn, (((0,), (0,)), ((), ())), preferred_element_type=jnp.float32)
            left[place, part * TILE : (part + 1) * TILE, :] = turned.astype(jnp.bfloat16)
        for c in range(count):
            right[place, c] = jnp.where(chan == c, piece, jnp.zeros_like(piece))

    def copies(step):
        slot = lax.rem(step, slots)
        tiles = pl.ds(step * together, together)
        return [
            pltpu.make_async_copy(buf.at[slot, c], out_ref.at[chunk * count + c, tiles], sem.at[slot, c])
            for c in range(count)
        ]

    def body(step, carry):
        slot = lax.rem(step, slots)

        @pl.when(step >= slots)
        def _():
            for done in copies(step - slots):
                done.wait()

        pairs = [(table_ref[step * together + u, 0], table_ref[step * together + u, 1]) for u in range(together)]
        for c, ready in enumerate(copies(step)):
            for u, (p, q) in enumerate(pairs):
                for part in range(2):
                    first = left[p, part * TILE : (part + 1) * TILE, :]
                    power = jnp.dot(first, right[q, c], preferred_element_type=jnp.float32)
                    buf[slot, c, u, part] = power.astype(jnp.bfloat16)
            ready.start()
        return carry

    lax.fori_loop(0, steps, body, 0)

    def drain(step, carry):
        for done in copies(step):
            done.wait()
        return carry

    lax.fori_loop(steps - slots, steps, drain, 0)


def cross_power(table, own, other, count, total, chunk, previous):
    depth, width = own.shape
    tiles = table.shape[0]
    together = 3 if tiles % 3 == 0 else 1
    vmem = pl.BlockSpec(memory_space=pltpu.VMEM)
    hbm = pl.BlockSpec(memory_space=pl.ANY)
    in_specs = [pl.BlockSpec(memory_space=pltpu.SMEM), vmem, vmem]
    args = [table, own, other]
    aliases = {}
    if previous is not None:
        in_specs.append(hbm)
        args.append(previous)
        aliases = {3: 0}
    return pl.pallas_call(
        functools.partial(power_kernel, count, chunk, together),
        in_specs=in_specs,
        out_specs=hbm,
        out_shape=jax.ShapeDtypeStruct((total, tiles, 2, TILE, TILE), jnp.bfloat16),
        scratch_shapes=[
            pltpu.VMEM((NB, 2 * TILE, depth), jnp.bfloat16),
            pltpu.VMEM((NB, count, depth, TILE), jnp.bfloat16),
            pltpu.VMEM((3, count, together, 2, TILE, TILE), jnp.bfloat16),
            pltpu.SemaphoreType.DMA((3, count)),
        ],
        input_output_aliases=aliases,
        compiler_params=params(32),
        cost_estimate=cost(2 * tiles * count * 2 * TILE * TILE * 256, tiles * count * 4 * TILE * TILE),
    )(*args)


def finish(table, own, count, total, chunk, out):
    other = lax.ppermute(own, "inp", [(0, 1), (1, 0)])
    return cross_power(table, own, other, count, total, chunk, out)


def turn_whole(samples, window, table, owners, total):
    inputs = samples.shape[0]
    cols = 2 * total
    together = 1 if cols % 8 == 0 else 8 // cols
    group = cols * together
    segments = [(0, d) for d in range(owners // together)]
    (partial,) = transform(samples, window, owners, 1, total, group, segments, [len(segments)])
    partial = partial.reshape(owners // together, TAPS, together, cols, inputs)
    partial = jnp.transpose(partial, (0, 2, 1, 3, 4)).reshape(owners, TAPS * cols, inputs)
    turned = lax.all_to_all(partial, "tm", split_axis=0, concat_axis=0, tiled=True)
    kernel = functools.partial(tap_sum_kernel, owners, total)
    sums = jax.ShapeDtypeStruct((cols * owners, inputs), jnp.bfloat16)
    (own,) = small(kernel, [sums], [turned.reshape(-1, inputs)])
    return finish(table, own, total, total, 0, None)


def local(raw_samples, pfb_window, tile_table):
    owners = lax.axis_size("tm")
    total = CHAN // owners
    if owners != 8:
        return turn_whole(raw_samples, pfb_window, tile_table, owners, total)

    inputs = raw_samples.shape[0]
    count = total // 2
    half = owners // 2
    segments = [(0, half + d) for d in range(half)]
    for d in range(half):
        segments += [(0, d), (1, d), (1, half + d)]
    outs = [1] * half + [3] * half
    sent = transform(raw_samples, pfb_window, owners, 2, count, 2 * count, segments, outs)

    def swap(block, d):
        return block if d == 0 else lax.ppermute(block, "tm", [(i, i ^ d) for i in range(owners)])

    far = [swap(sent[d], half + d) for d in range(half)]
    near = [swap(sent[half + d], d) for d in range(half)]
    exact = jax.ShapeDtypeStruct((2 * count * owners, inputs), jnp.float32)
    rounded = jax.ShapeDtypeStruct((2 * count * owners, inputs), jnp.bfloat16)
    kernel = functools.partial(near_sum_kernel, owners, count)
    near_first, near_second, facing = small(kernel, [exact, exact, rounded], near)
    faced = swap(facing, half)
    kernel = functools.partial(far_sum_kernel, owners, count)
    (own,) = small(kernel, [rounded], [near_first] + far)
    out = finish(tile_table, own, count, total, 0, None)
    faced, out = lax.optimization_barrier((faced, out))
    (own,) = small(join_kernel, [rounded], [near_second, faced])
    return finish(tile_table, own, count, total, 1, out)


def solution(mesh):
    return jax.shard_map(
        local,
        mesh=mesh,
        in_specs=(P(("grp", "inp"), "tm"), P(), P("inp", None)),
        out_specs=P(("grp", "tm"), "inp", None, None, None),
        check_vma=False,
    )
```

```python
import functools

import jax
import jax.numpy as jnp
import numpy as np
from jax import lax
from jax.experimental import pallas as pl
from jax.experimental.pallas import tpu as pltpu
from jax.sharding import PartitionSpec as P

INPUTS = 2048
NFFT = 2048
TAPS = 4
CHAN = 64
TILE = 256
NB = INPUTS // TILE
SPLIT = 4
ORDERS = ((0, 1, 2, 3), (0, 3, 2, 1))
TERMS = (1, 2)
BLOCKS = 1
HALF = NB // 2


def params(mib):
    return pltpu.CompilerParams(vmem_limit_bytes=mib << 20)


def cost(flops, moved):
    return pl.CostEstimate(flops=flops, transcendentals=0, bytes_accessed=moved)


def basis_rows(owners, first, count):
    per_owner = CHAN // owners
    chan = np.arange(owners)[:, None] * per_owner + first + np.arange(count)[None, :]
    wrapped = (np.arange(NFFT, dtype=np.int64)[None, :] * (CHAN + chan.reshape(-1, 1))) % NFFT
    angle = wrapped.astype(np.float64) * (2.0 * np.pi / NFFT)
    both = np.stack([np.cos(angle), -np.sin(angle)], axis=1) / np.sqrt(NFFT)
    return both.reshape(-1, NFFT).astype(np.float32)


def transform_kernel(group, segments, basis_hbm, window_hbm, samples_hbm, *refs):
    *out_refs, basis, window, samples, weights, total, sems = refs
    terms = weights.shape[0]
    depth = NFFT // SPLIT
    pieces = [pl.ds(k * depth, depth) for k in range(SPLIT)]
    copies = [pltpu.make_async_copy(window_hbm, window, sems.at[2 * SPLIT])]
    for k, piece in enumerate(pieces):
        copies.append(pltpu.make_async_copy(basis_hbm.at[:, piece], basis.at[:, piece], sems.at[2 * k]))
        copies.append(pltpu.make_async_copy(samples_hbm.at[:, piece], samples.at[:, piece], sems.at[2 * k + 1]))
    for copy in copies:
        copy.start()
    copies[0].wait()
    size = samples.shape[0] // BLOCKS
    for k, piece in enumerate(pieces):
        copies[1 + 2 * k].wait()
        for index, distance in enumerate(segments):
            place = distance
            if len(out_refs) > 1:
                place = lax.bitwise_xor(lax.axis_index("tm"), distance)
            rows = basis[pl.ds(pl.multiple_of(place * group, group), group), piece]
            product = jnp.concatenate([rows * window[t : t + 1, piece] for t in range(TAPS)], axis=0)
            for term in range(terms):
                rounded = product.astype(jnp.bfloat16)
                weights[term, pl.ds(index * group * TAPS, group * TAPS), piece] = rounded
                product -= rounded.astype(jnp.float32)
        copies[2 + 2 * k].wait()
        for b in range(BLOCKS):
            columns = pl.ds(b * size, size)
            contract = (((1,), (1,)), ((), ()))
            part = total[:, columns] if k else 0.0
            for term in range(terms):
                part += lax.dot_general(
                    weights[term, :, piece], samples[columns, piece], contract, preferred_element_type=jnp.float32
                )
            if k < SPLIT - 1:
                total[:, columns] = part
                continue
            part = part.astype(jnp.bfloat16)
            first = 0
            for out_ref in out_refs:
                out_ref[:, columns] = part[first : first + out_ref.shape[0]]
                first += out_ref.shape[0]


def transform(samples, window, owners, first, count, group, segments, outs, terms):
    inputs = samples.shape[0]
    basis = basis_rows(owners, first, count)
    rows = len(segments) * group * TAPS
    hbm = pl.BlockSpec(memory_space=pl.ANY)
    return pl.pallas_call(
        functools.partial(transform_kernel, group, segments),
        in_specs=[hbm] * 3,
        out_specs=[pl.BlockSpec(memory_space=pltpu.VMEM)] * len(outs),
        out_shape=[jax.ShapeDtypeStruct((n * group * TAPS, inputs), jnp.bfloat16) for n in outs],
        scratch_shapes=[
            pltpu.VMEM(basis.shape, jnp.float32),
            pltpu.VMEM((TAPS, NFFT), jnp.float32),
            pltpu.VMEM((inputs, NFFT), jnp.bfloat16),
            pltpu.VMEM((terms, rows, NFFT), jnp.bfloat16),
            pltpu.VMEM((rows, inputs), jnp.float32),
            pltpu.SemaphoreType.DMA((2 * SPLIT + 1,)),
        ],
        compiler_params=params(40),
        cost_estimate=cost(2 * terms * rows * inputs * NFFT, 8 << 20),
    )(*[pltpu.with_memory_space_constraint(a, pltpu.HBM) for a in (jnp.asarray(basis), window, samples)])


def tap_matrix(frames, pieces, count, first):
    cols = 2 * count
    shape = (cols * frames, pieces * TAPS * cols)
    row = lax.broadcasted_iota(jnp.int32, shape, 0)
    col = lax.broadcasted_iota(jnp.int32, shape, 1)
    source = lax.bitwise_xor(col // (TAPS * cols), first)
    hit = (col % cols == row // frames) & (row % frames - (col // cols) % TAPS == source)
    return jnp.where(hit, 1.0, 0.0).astype(jnp.bfloat16)


def tap_sum_kernel(owners, count, spectra_ref, out_ref):
    add = tap_matrix(owners, owners, count, 0)
    out_ref[...] = jnp.dot(add, spectra_ref[...], preferred_element_type=jnp.float32).astype(jnp.bfloat16)


def near_sum_kernel(owners, count, order, *refs):
    *parts, mine, facing = refs
    parts = [parts[order.index(d)] for d in range(len(parts))]
    depth = TAPS * 2 * count
    add = tap_matrix(owners, owners // 2, count, lax.axis_index("tm"))
    for index, out_ref in enumerate((mine, facing)):
        spectra = jnp.concatenate([ref[index * depth : (index + 1) * depth, :] for ref in parts], axis=0)
        total = jnp.dot(add, spectra, preferred_element_type=jnp.float32)
        out_ref[...] = total.astype(out_ref.dtype)


def join_kernel(near_ref, far_ref, out_ref):
    out_ref[...] = (near_ref[...] + far_ref[...].astype(jnp.float32)).astype(jnp.bfloat16)


def small(kernel, outs, inputs, flops=1 << 28):
    vmem = pl.BlockSpec(memory_space=pltpu.VMEM)
    return pl.pallas_call(
        kernel,
        in_specs=[vmem] * len(inputs),
        out_specs=[vmem] * len(outs),
        out_shape=outs,
        compiler_params=params(16),
        cost_estimate=cost(flops, 1 << 20),
    )(*inputs)


def power_kernel(count, chunk, together, table_ref, own_ref, other_ref, *refs):
    out_ref, left, right, buf, sem = refs[-5:]
    depth = own_ref.shape[0]
    frames = depth // (2 * count)
    slots = buf.shape[0]
    steps = out_ref.shape[1] // together
    mine = lax.axis_index("inp") * HALF

    row = lax.broadcasted_iota(jnp.int32, (depth, depth), 0)
    col = lax.broadcasted_iota(jnp.int32, (depth, depth), 1)
    scale = 1.0 / frames
    real = jnp.where(row == col, scale, 0.0).astype(jnp.bfloat16)
    sign = jnp.where((col // frames) % 2 == 0, scale, -scale)
    partner = (row // (2 * frames) == col // (2 * frames)) & (row % frames == col % frames)
    imag = jnp.where(partner & (row != col), sign, 0.0).astype(jnp.bfloat16)
    chan = lax.broadcasted_iota(jnp.int32, (depth, TILE), 0) // (2 * frames)
    for index in range(NB):
        ref = own_ref if index < HALF else other_ref
        place = (mine if index < HALF else HALF - mine) + index % HALF
        piece = ref[:, (index % HALF) * TILE : (index % HALF + 1) * TILE]
        for part, turn in enumerate((real, imag)):
            turned = lax.dot_general(piece, turn, (((0,), (0,)), ((), ())), preferred_element_type=jnp.float32)
            left[place, part * TILE : (part + 1) * TILE, :] = turned.astype(jnp.bfloat16)
        for c in range(count):
            right[place, c] = jnp.where(chan == c, piece, jnp.zeros_like(piece))

    def copies(step):
        slot = lax.rem(step, slots)
        tiles = pl.ds(step * together, together)
        return [
            pltpu.make_async_copy(buf.at[slot, c], out_ref.at[chunk * count + c, tiles], sem.at[slot, c])
            for c in range(count)
        ]

    def body(step, carry):
        slot = lax.rem(step, slots)

        @pl.when(step >= slots)
        def _():
            for done in copies(step - slots):
                done.wait()

        pairs = [(table_ref[step * together + u, 0], table_ref[step * together + u, 1]) for u in range(together)]
        for c, ready in enumerate(copies(step)):
            for u, (p, q) in enumerate(pairs):
                for part in range(2):
                    first = left[p, part * TILE : (part + 1) * TILE, :]
                    power = jnp.dot(first, right[q, c], preferred_element_type=jnp.float32)
                    buf[slot, c, u, part] = power.astype(jnp.bfloat16)
            ready.start()
        return carry

    lax.fori_loop(0, steps, body, 0)

    def drain(step, carry):
        for done in copies(step):
            done.wait()
        return carry

    lax.fori_loop(steps - slots, steps, drain, 0)


def cross_power(table, own, other, count, total, chunk, previous):
    depth, width = own.shape
    tiles = table.shape[0]
    together = 3 if tiles % 3 == 0 else 1
    vmem = pl.BlockSpec(memory_space=pltpu.VMEM)
    hbm = pl.BlockSpec(memory_space=pl.ANY)
    in_specs = [pl.BlockSpec(memory_space=pltpu.SMEM), vmem, vmem]
    args = [table, own, other]
    aliases = {}
    if previous is not None:
        in_specs.append(hbm)
        args.append(previous)
        aliases = {3: 0}
    return pl.pallas_call(
        functools.partial(power_kernel, count, chunk, together),
        in_specs=in_specs,
        out_specs=hbm,
        out_shape=jax.ShapeDtypeStruct((total, tiles, 2, TILE, TILE), jnp.bfloat16),
        scratch_shapes=[
            pltpu.VMEM((NB, 2 * TILE, depth), jnp.bfloat16),
            pltpu.VMEM((NB, count, depth, TILE), jnp.bfloat16),
            pltpu.VMEM((3, count, together, 2, TILE, TILE), jnp.bfloat16),
            pltpu.SemaphoreType.DMA((3, count)),
        ],
        input_output_aliases=aliases,
        compiler_params=params(32),
        cost_estimate=cost(1 << 28, 1 << 20),
    )(*args)


def finish(table, own, count, total, chunk, out):
    other = lax.ppermute(own, "inp", [(0, 1), (1, 0)])
    return cross_power(table, own, other, count, total, chunk, out)


def turn_whole(samples, window, table, owners, total):
    inputs = samples.shape[0]
    cols = 2 * total
    together = 1 if cols % 8 == 0 else 8 // cols
    group = cols * together
    segments = list(range(owners // together))
    (partial,) = transform(samples, window, owners, 0, total, group, segments, [len(segments)], 2)
    partial = partial.reshape(owners // together, TAPS, together, cols, inputs)
    partial = jnp.transpose(partial, (0, 2, 1, 3, 4)).reshape(owners, TAPS * cols, inputs)
    turned = lax.all_to_all(partial, "tm", split_axis=0, concat_axis=0, tiled=True)
    kernel = functools.partial(tap_sum_kernel, owners, total)
    sums = jax.ShapeDtypeStruct((cols * owners, inputs), jnp.bfloat16)
    (own,) = small(kernel, [sums], [turned.reshape(-1, inputs)])
    return finish(table, own, total, total, 0, None)


def local(raw_samples, pfb_window, tile_table):
    owners = lax.axis_size("tm")
    total = CHAN // owners
    if owners != 8:
        return turn_whole(raw_samples, pfb_window, tile_table, owners, total)

    inputs = raw_samples.shape[0]
    count = total // 2
    half = owners // 2
    segments = [d + far for d in range(half) for far in (0, half)]

    def swap(block, d):
        return block if d == 0 else lax.ppermute(block, "tm", [(i, i ^ d) for i in range(owners)])

    exact = jax.ShapeDtypeStruct((2 * count * owners, inputs), jnp.float32)
    rounded = jax.ShapeDtypeStruct((2 * count * owners, inputs), jnp.bfloat16)
    parts = [
        transform(raw_samples, pfb_window, owners, chunk * count, count, 2 * count, segments, [2] * half, TERMS[chunk])
        for chunk in range(2)
    ]
    near = [swap(parts[0][d], d) for d in ORDERS[0]]
    near, parts[1] = lax.optimization_barrier((near, parts[1]))
    sums = []
    for chunk in range(2):
        if chunk:
            near = [swap(parts[1][d], d) for d in ORDERS[1]]
        kernel = functools.partial(near_sum_kernel, owners, count, ORDERS[chunk])
        mine, facing = small(kernel, [exact, rounded], near)
        sums.append((mine, swap(facing, half)))
    out = None
    for chunk, (mine, faced) in enumerate(sums):
        if out is not None:
            faced, out = lax.optimization_barrier((faced, out))
        (own,) = small(join_kernel, [rounded], [mine, faced], 1 << 34)
        out = finish(tile_table, own, count, total, chunk, out)
    return out


def solution(mesh):
    return jax.shard_map(
        local,
        mesh=mesh,
        in_specs=(P(("grp", "inp"), "tm"), P(), P("inp", None)),
        out_specs=P(("grp", "tm"), "inp", None, None, None),
        check_vma=False,
    )
```

```python
import functools

import jax
import jax.numpy as jnp
import numpy as np
from jax import lax
from jax.experimental import pallas as pl
from jax.experimental.pallas import tpu as pltpu
from jax.sharding import PartitionSpec as P

INPUTS = 2048
NFFT = 2048
TAPS = 4
CHAN = 64
TILE = 256
NB = INPUTS // TILE
SPLIT = 4
ORDERS = ((0, 1, 2, 3), (0, 3, 2, 1))
TERMS = (1, 2)
BLOCKS = 1
HALF = NB // 2


def params(mib):
    return pltpu.CompilerParams(vmem_limit_bytes=mib << 20)


def cost(flops, moved):
    return pl.CostEstimate(flops=flops, transcendentals=0, bytes_accessed=moved)


def basis_rows(owners, first, count):
    per_owner = CHAN // owners
    chan = np.arange(owners)[:, None] * per_owner + first + np.arange(count)[None, :]
    wrapped = (np.arange(NFFT, dtype=np.int64)[None, :] * (CHAN + chan.reshape(-1, 1))) % NFFT
    angle = wrapped.astype(np.float64) * (2.0 * np.pi / NFFT)
    both = np.stack([np.cos(angle), -np.sin(angle)], axis=1) / np.sqrt(NFFT)
    return both.reshape(-1, NFFT).astype(np.float32)


def transform_kernel(group, segments, basis_hbm, window_hbm, samples_hbm, *refs):
    *out_refs, basis, window, samples, weights, total, sems = refs
    terms = weights.shape[0]
    depth = NFFT // SPLIT
    pieces = [pl.ds(k * depth, depth) for k in range(SPLIT)]
    copies = [pltpu.make_async_copy(window_hbm, window, sems.at[2 * SPLIT])]
    for k, piece in enumerate(pieces):
        copies.append(pltpu.make_async_copy(basis_hbm.at[:, piece], basis.at[:, piece], sems.at[2 * k]))
        copies.append(pltpu.make_async_copy(samples_hbm.at[:, piece], samples.at[:, piece], sems.at[2 * k + 1]))
    for copy in copies:
        copy.start()
    copies[0].wait()
    size = samples.shape[0] // BLOCKS
    for k, piece in enumerate(pieces):
        copies[1 + 2 * k].wait()
        for index, distance in enumerate(segments):
            place = distance
            if len(out_refs) > 1:
                place = lax.bitwise_xor(lax.axis_index("tm"), distance)
            rows = basis[pl.ds(pl.multiple_of(place * group, group), group), piece]
            product = jnp.concatenate([rows * window[t : t + 1, piece] for t in range(TAPS)], axis=0)
            for term in range(terms):
                rounded = product.astype(jnp.bfloat16)
                weights[term, pl.ds(index * group * TAPS, group * TAPS), piece] = rounded
                product -= rounded.astype(jnp.float32)
        copies[2 + 2 * k].wait()
        for b in range(BLOCKS):
            columns = pl.ds(b * size, size)
            contract = (((1,), (1,)), ((), ()))
            part = total[:, columns] if k else 0.0
            for term in range(terms):
                part += lax.dot_general(
                    weights[term, :, piece], samples[columns, piece], contract, preferred_element_type=jnp.float32
                )
            if k < SPLIT - 1:
                total[:, columns] = part
                continue
            part = part.astype(jnp.bfloat16)
            first = 0
            for out_ref in out_refs:
                out_ref[:, columns] = part[first : first + out_ref.shape[0]]
                first += out_ref.shape[0]


def transform(samples, window, owners, first, count, group, segments, outs, terms):
    inputs = samples.shape[0]
    basis = basis_rows(owners, first, count)
    rows = len(segments) * group * TAPS
    hbm = pl.BlockSpec(memory_space=pl.ANY)
    return pl.pallas_call(
        functools.partial(transform_kernel, group, segments),
        in_specs=[hbm] * 3,
        out_specs=[pl.BlockSpec(memory_space=pltpu.VMEM)] * len(outs),
        out_shape=[jax.ShapeDtypeStruct((n * group * TAPS, inputs), jnp.bfloat16) for n in outs],
        scratch_shapes=[
            pltpu.VMEM(basis.shape, jnp.float32),
            pltpu.VMEM((TAPS, NFFT), jnp.float32),
            pltpu.VMEM((inputs, NFFT), jnp.bfloat16),
            pltpu.VMEM((terms, rows, NFFT), jnp.bfloat16),
            pltpu.VMEM((rows, inputs), jnp.float32),
            pltpu.SemaphoreType.DMA((2 * SPLIT + 1,)),
        ],
        compiler_params=params(40),
        cost_estimate=cost(2 * terms * rows * inputs * NFFT, 8 << 20),
    )(*[pltpu.with_memory_space_constraint(a, pltpu.HBM) for a in (jnp.asarray(basis), window, samples)])


def tap_matrix(frames, pieces, count, first):
    cols = 2 * count
    shape = (cols * frames, pieces * TAPS * cols)
    row = lax.broadcasted_iota(jnp.int32, shape, 0)
    col = lax.broadcasted_iota(jnp.int32, shape, 1)
    source = lax.bitwise_xor(col // (TAPS * cols), first)
    hit = (col % cols == row // frames) & (row % frames - (col // cols) % TAPS == source)
    return jnp.where(hit, 1.0, 0.0).astype(jnp.bfloat16)


def tap_sum_kernel(owners, count, spectra_ref, out_ref):
    add = tap_matrix(owners, owners, count, 0)
    out_ref[...] = jnp.dot(add, spectra_ref[...], preferred_element_type=jnp.float32).astype(jnp.bfloat16)


def near_sum_kernel(owners, count, order, *refs):
    *parts, mine, facing = refs
    parts = [parts[order.index(d)] for d in range(len(parts))]
    depth = TAPS * 2 * count
    add = tap_matrix(owners, owners // 2, count, lax.axis_index("tm"))
    for index, out_ref in enumerate((mine, facing)):
        spectra = jnp.concatenate([ref[index * depth : (index + 1) * depth, :] for ref in parts], axis=0)
        total = jnp.dot(add, spectra, preferred_element_type=jnp.float32)
        out_ref[...] = total.astype(out_ref.dtype)


def join_kernel(near_ref, far_ref, out_ref):
    out_ref[...] = (near_ref[...] + far_ref[...].astype(jnp.float32)).astype(jnp.bfloat16)


def small(kernel, outs, inputs, flops=1 << 28):
    vmem = pl.BlockSpec(memory_space=pltpu.VMEM)
    return pl.pallas_call(
        kernel,
        in_specs=[vmem] * len(inputs),
        out_specs=[vmem] * len(outs),
        out_shape=outs,
        compiler_params=params(16),
        cost_estimate=cost(flops, 1 << 20),
    )(*inputs)


def power_kernel(count, chunk, together, table_ref, own_ref, other_ref, *refs):
    out_ref, left, right, buf, sem = refs[-5:]
    depth = own_ref.shape[0]
    frames = depth // (2 * count)
    slots = buf.shape[0]
    steps = out_ref.shape[1] // together
    mine = lax.axis_index("inp") * HALF

    row = lax.broadcasted_iota(jnp.int32, (depth, depth), 0)
    col = lax.broadcasted_iota(jnp.int32, (depth, depth), 1)
    scale = 1.0 / frames
    real = jnp.where(row == col, scale, 0.0).astype(jnp.bfloat16)
    sign = jnp.where((col // frames) % 2 == 0, scale, -scale)
    partner = (row // (2 * frames) == col // (2 * frames)) & (row % frames == col % frames)
    imag = jnp.where(partner & (row != col), sign, 0.0).astype(jnp.bfloat16)
    chan = lax.broadcasted_iota(jnp.int32, (depth, TILE), 0) // (2 * frames)
    for index in range(NB):
        ref = own_ref if index < HALF else other_ref
        place = (mine if index < HALF else HALF - mine) + index % HALF
        piece = ref[:, (index % HALF) * TILE : (index % HALF + 1) * TILE]
        for part, turn in enumerate((real, imag)):
            turned = lax.dot_general(piece, turn, (((0,), (0,)), ((), ())), preferred_element_type=jnp.float32)
            left[place, part * TILE : (part + 1) * TILE, :] = turned.astype(jnp.bfloat16)
        for c in range(count):
            right[place, c] = jnp.where(chan == c, piece, jnp.zeros_like(piece))

    def copies(step):
        slot = lax.rem(step, slots)
        tiles = pl.ds(step * together, together)
        return [
            pltpu.make_async_copy(buf.at[slot, c], out_ref.at[chunk * count + c, tiles], sem.at[slot, c])
            for c in range(count)
        ]

    def body(step, carry):
        slot = lax.rem(step, slots)

        @pl.when(step >= slots)
        def _():
            for done in copies(step - slots):
                done.wait()

        pairs = [(table_ref[step * together + u, 0], table_ref[step * together + u, 1]) for u in range(together)]
        for c, ready in enumerate(copies(step)):
            for u, (p, q) in enumerate(pairs):
                for quarter in range(4):
                    rows = pl.ds(quarter % 2 * (TILE // 2), TILE // 2)
                    first = left[p, quarter * TILE // 2 : (quarter + 1) * TILE // 2, :]
                    power = jnp.dot(first, right[q, c], preferred_element_type=jnp.float32)
                    buf[slot, c, u, quarter // 2, rows] = power.astype(jnp.bfloat16)
            ready.start()
        return carry

    lax.fori_loop(0, steps, body, 0)

    def drain(step, carry):
        for done in copies(step):
            done.wait()
        return carry

    lax.fori_loop(steps - slots, steps, drain, 0)


def cross_power(table, own, other, count, total, chunk, previous):
    depth, width = own.shape
    tiles = table.shape[0]
    together = 3 if tiles % 3 == 0 else 1
    vmem = pl.BlockSpec(memory_space=pltpu.VMEM)
    hbm = pl.BlockSpec(memory_space=pl.ANY)
    in_specs = [pl.BlockSpec(memory_space=pltpu.SMEM), vmem, vmem]
    args = [table, own, other]
    aliases = {}
    if previous is not None:
        in_specs.append(hbm)
        args.append(previous)
        aliases = {3: 0}
    return pl.pallas_call(
        functools.partial(power_kernel, count, chunk, together),
        in_specs=in_specs,
        out_specs=hbm,
        out_shape=jax.ShapeDtypeStruct((total, tiles, 2, TILE, TILE), jnp.bfloat16),
        scratch_shapes=[
            pltpu.VMEM((NB, 2 * TILE, depth), jnp.bfloat16),
            pltpu.VMEM((NB, count, depth, TILE), jnp.bfloat16),
            pltpu.VMEM((3, count, together, 2, TILE, TILE), jnp.bfloat16),
            pltpu.SemaphoreType.DMA((3, count)),
        ],
        input_output_aliases=aliases,
        compiler_params=params(32),
        cost_estimate=cost(1 << 28, 1 << 20),
    )(*args)


def finish(table, own, count, total, chunk, out):
    other = lax.ppermute(own, "inp", [(0, 1), (1, 0)])
    return cross_power(table, own, other, count, total, chunk, out)


def turn_whole(samples, window, table, owners, total):
    inputs = samples.shape[0]
    cols = 2 * total
    together = 1 if cols % 8 == 0 else 8 // cols
    group = cols * together
    segments = list(range(owners // together))
    (partial,) = transform(samples, window, owners, 0, total, group, segments, [len(segments)], 2)
    partial = partial.reshape(owners // together, TAPS, together, cols, inputs)
    partial = jnp.transpose(partial, (0, 2, 1, 3, 4)).reshape(owners, TAPS * cols, inputs)
    turned = lax.all_to_all(partial, "tm", split_axis=0, concat_axis=0, tiled=True)
    kernel = functools.partial(tap_sum_kernel, owners, total)
    sums = jax.ShapeDtypeStruct((cols * owners, inputs), jnp.bfloat16)
    (own,) = small(kernel, [sums], [turned.reshape(-1, inputs)])
    return finish(table, own, total, total, 0, None)


def local(raw_samples, pfb_window, tile_table):
    owners = lax.axis_size("tm")
    total = CHAN // owners
    if owners != 8:
        return turn_whole(raw_samples, pfb_window, tile_table, owners, total)

    inputs = raw_samples.shape[0]
    count = total // 2
    half = owners // 2
    segments = [d + far for d in range(half) for far in (0, half)]

    def swap(block, d):
        return block if d == 0 else lax.ppermute(block, "tm", [(i, i ^ d) for i in range(owners)])

    exact = jax.ShapeDtypeStruct((2 * count * owners, inputs), jnp.float32)
    rounded = jax.ShapeDtypeStruct((2 * count * owners, inputs), jnp.bfloat16)
    parts = [
        transform(raw_samples, pfb_window, owners, chunk * count, count, 2 * count, segments, [2] * half, TERMS[chunk])
        for chunk in range(2)
    ]
    near = [swap(parts[0][d], d) for d in ORDERS[0]]
    near, parts[1] = lax.optimization_barrier((near, parts[1]))
    sums = []
    for chunk in range(2):
        if chunk:
            near = [swap(parts[1][d], d) for d in ORDERS[1]]
        kernel = functools.partial(near_sum_kernel, owners, count, ORDERS[chunk])
        mine, facing = small(kernel, [exact, rounded], near)
        sums.append((mine, swap(facing, half)))
    out = None
    for chunk, (mine, faced) in enumerate(sums):
        if out is not None:
            faced, out = lax.optimization_barrier((faced, out))
        (own,) = small(join_kernel, [rounded], [mine, faced], 1 << 34)
        out = finish(tile_table, own, count, total, chunk, out)
    return out


def solution(mesh):
    return jax.shard_map(
        local,
        mesh=mesh,
        in_specs=(P(("grp", "inp"), "tm"), P(), P("inp", None)),
        out_specs=P(("grp", "tm"), "inp", None, None, None),
        check_vma=False,
    )
```
